32 devices in a mesh: dp: 8 (over y, x, core), tensor: 4 (over z).
Axes of the slice: x: 2, y: 2, z: 4, core: 2. Of those that a mesh axis runs over, the one named last changes fastest.
Arguments:
- inputs: bfloat16 [1, 16384, 768], P(None, ('dp', 'tensor')), may hold values from -6 to 6
- lengths: int32 [8, 1, 4], P('dp'), may hold values from 1 to 2045, as said below
- w_qkv: bfloat16 [3, 768, 768], P(None, 'dp', 'tensor'), may hold values from -0.21875 to 0.21875
- b_qv: bfloat16 [2, 768], P(None, 'tensor'), may hold values from -3 to 3
- w_out: bfloat16 [768, 768], P('tensor', 'dp'), may hold values from -0.875 to 0.875
- b_out: bfloat16 [768], replicated, may hold values from -3 to 3
- w_fc: bfloat16 [768, 3072], P('dp', 'tensor'), may hold values from -0.21875 to 0.21875
- b_fc: bfloat16 [3072], P('tensor'), may hold values from -3 to 3
- w_proj: bfloat16 [3072, 768], P('tensor', 'dp'), may hold values from -0.109375 to 0.109375
- b_proj: bfloat16 [768], replicated, may hold values from -3 to 3
- gain_one: bfloat16 [768], replicated, may hold values from 0.5 to 1.5
- shift_one: bfloat16 [768], replicated, may hold values from -2 to 2
- gain_two: bfloat16 [768], replicated, may hold values from 0.5 to 1.5
- shift_two: bfloat16 [768], replicated, may hold values from -2 to 2
- cotangent: bfloat16 [1, 16384, 768], P(None, ('dp', 'tensor')), may hold values from -6 to 6
Outputs:
- output: bfloat16 [1, 16384, 768], P(None, ('dp', 'tensor'))
- grad_inputs: float32 [1, 16384, 768], P(None, ('dp', 'tensor'))
- d_w_qkv: float32 [3, 768, 768], P(None, 'dp', 'tensor')
- d_b_qv: float32 [2, 768], P(None, 'tensor')
- d_w_out: float32 [768, 768], P('tensor', 'dp')
- d_b_out: float32 [768], replicated
- d_w_fc: float32 [768, 3072], P('dp', 'tensor')
- d_b_fc: float32 [3072], P('tensor')
- d_w_proj: float32 [3072, 768], P('tensor', 'dp')
- d_b_proj: float32 [768], replicated
- d_gain_one: float32 [768], replicated
- d_shift_one: float32 [768], replicated
- d_gain_two: float32 [768], replicated
- d_shift_two: float32 [768], replicated
The draws below stay inside these ranges and needn't reach their ends.
Inputs may be any that keep to these rules, and one draw needn't show every extreme that they name: The 4 lengths of one pack sum to at most 2048.
All inputs are finite; a program needn't handle non-finite values.
Results may differ from the reference program's by a relative error of at most 0.0098.
Values may be sent and summed in bfloat16 or wider, within the bound.
No kernel may reach another device: no remote copies, remote signals or barrier semaphores. Data moves between devices by JAX's collectives and lax.ppermute only.
A program may use at most 192 MiB of HBM per device.

```python
from functools import partial
import jax
import jax.numpy as jnp
from jax import lax

D = 768
HEADS = 12
HEAD_DIM = 64
FF = 3072
PACK_LEN = 2048
SEQS = 4
PACKS = 1
ROWS = 16384
N_DP = 8


def draw_lengths(key, part):
    key = jax.random.fold_in(key, 11)
    short_key, long_key, chosen_key = jax.random.split(key, 3)
    most_short = PACK_LEN // (4 * (SEQS - 1))
    shorts = jax.random.randint(short_key, (N_DP, PACKS, SEQS - 1), 1, most_short + 1)
    first_pack = (jnp.arange(N_DP, dtype=jnp.int32)[:, None] == 0) & (jnp.arange(PACKS, dtype=jnp.int32)[None, :] == 0)
    shorts = jnp.where(first_pack[..., None], 1, shorts)
    least_long = 3 * PACK_LEN // 4 + 1
    spare_room = PACK_LEN - jnp.sum(shorts, axis=-1) - least_long + 1
    longest = least_long + jax.random.randint(long_key, (N_DP, PACKS), 0, spare_room)
    longest = jnp.where(first_pack, PACK_LEN - SEQS + 1, longest)
    chosen = jax.random.randint(chosen_key, (N_DP, PACKS, 1), 0, SEQS)
    places = jnp.arange(SEQS, dtype=jnp.int32)[None, None, :]
    source = jnp.clip(places - (places > chosen).astype(jnp.int32), 0, SEQS - 2)
    picked = jnp.take_along_axis(shorts, source, axis=-1)
    return jnp.where(places == chosen, longest[..., None], picked).astype(jnp.int32)


def shard_levels(rng, extent, pieces, low, largest):
    loudness = 1.0
    for dim, parts in pieces:
        heights = jax.random.uniform(jax.random.fold_in(jax.random.fold_in(rng, 6), dim), (parts,), jnp.float32, low / len(pieces), largest / len(pieces))
        loudness = loudness * jnp.repeat(jnp.exp(heights), extent[dim] // parts).reshape((-1,) + (1,) * (len(extent) - 1 - dim))
    return loudness


def scatter_about(key, extent, width, most, pieces=(), kind=jnp.bfloat16):
    values = jax.random.normal(key, extent, jnp.float32) * width
    if len(pieces) > 0:
        values = shard_levels(key, extent, pieces, -0.22, 0.18) * values
    return jnp.clip(values, min=-most, max=most).astype(kind)


def setup_inputs(seed: int = 0) -> dict:
    seeds = jax.random.split(jax.random.key(seed), 16)
    inputs = scatter_about(seeds[0], (PACKS, ROWS, D), 1.0, 6.0, ((1, 32),))
    lengths = draw_lengths(jax.random.fold_in(seeds[15], 71), 0)
    w_qkv = scatter_about(seeds[2], (3, D, D), D ** -0.5, 0.21875, ((1, 8), (2, 4)))
    b_qv = scatter_about(seeds[3], (2, D), 0.5, 3.0, ((1, 4),))
    w_out = scatter_about(seeds[4], (D, D), (D // 16) ** -0.5, 0.875, ((0, 4), (1, 8)))
    b_out = scatter_about(seeds[5], (D,), 0.5, 3.0)
    w_fc = scatter_about(seeds[6], (D, FF), D ** -0.5, 0.21875, ((0, 8), (1, 4)))
    b_fc = scatter_about(seeds[7], (FF,), 0.5, 3.0, ((0, 4),))
    w_proj = scatter_about(seeds[8], (FF, D), FF ** -0.5, 0.109375, ((0, 4), (1, 8)))
    b_proj = scatter_about(seeds[9], (D,), 0.5, 3.0)
    gain_one = jnp.clip(1.0 + 0.1 * jax.random.normal(seeds[10], (D,), jnp.float32), 0.5, 1.5).astype(jnp.bfloat16)
    shift_one = scatter_about(seeds[11], (D,), 0.3, 2.0)
    gain_two = jnp.clip(1.0 + 0.1 * jax.random.normal(seeds[12], (D,), jnp.float32), 0.5, 1.5).astype(jnp.bfloat16)
    shift_two = scatter_about(seeds[13], (D,), 0.3, 2.0)
    cotangent = scatter_about(seeds[14], (PACKS, ROWS, D), 1.0, 6.0, ((1, 32),))
    return dict(inputs=inputs, lengths=lengths, w_qkv=w_qkv, b_qv=b_qv, w_out=w_out, b_out=b_out, w_fc=w_fc, b_fc=b_fc, w_proj=w_proj, b_proj=b_proj, gain_one=gain_one, shift_one=shift_one, gain_two=gain_two, shift_two=shift_two, cotangent=cotangent)


HIGHEST = lax.Precision.HIGHEST
EPSILON = 1e-05
MASKED = -1000000000.0

@jax.custom_vjp
def low(v):
    return lax.optimization_barrier(v.astype(jnp.bfloat16)).astype(jnp.float32)

@jax.custom_vjp
def low_back(v):
    return v

def low_keep(v):
    return (low(v), None)

def low_pass(kept, grad):
    return (grad,)

def back_keep(v):
    return (v, None)

def back_low(kept, grad):
    return (low(grad),)
low.defvjp(low_keep, low_pass)
low_back.defvjp(back_keep, back_low)

def norm_rows(row_vals, gain, shift):
    row_mean = lax.optimization_barrier(jnp.mean(row_vals, axis=-1, keepdims=True))
    centred = row_vals - row_mean
    spread = lax.optimization_barrier(jnp.mean(centred * centred, axis=-1, keepdims=True))
    return centred * lax.rsqrt(spread + EPSILON) * gain + shift

def doc_ids(pack_lengths):
    seq_ends = jnp.cumsum(pack_lengths, dtype=jnp.int32)
    places = jnp.arange(PACK_LEN, dtype=jnp.int32)
    passed = lax.optimization_barrier(jnp.sum((places[:, None] >= seq_ends[None, :]).astype(jnp.int32), axis=1, dtype=jnp.int32))
    return jnp.where(passed < SEQS, passed, SEQS + places)

def head_attend(allowed, operands):
    queries, key_rows, values = operands
    scores = low_back(jnp.dot(queries, key_rows.T, precision=HIGHEST) * HEAD_DIM ** (-0.5))
    scores = jnp.where(allowed, scores, MASKED)
    row_max = lax.optimization_barrier(jnp.max(scores, axis=-1, keepdims=True))
    exponent = jnp.exp(scores - row_max)
    attn_probs = exponent / lax.optimization_barrier(jnp.sum(exponent, axis=-1, keepdims=True))
    return jnp.dot(low(attn_probs), values, precision=HIGHEST)

def split_heads(rows_in):
    return rows_in.reshape(PACK_LEN, HEADS, HEAD_DIM).transpose(1, 0, 2)

def whole_layer(params, rows_in, allowed):
    w_qkv, b_qv, w_out, b_out, w_fc, b_fc, w_proj, b_proj, gain_one, shift_one, gain_two, shift_two = params
    h_one = low(norm_rows(rows_in, gain_one, shift_one))
    projected = jnp.einsum('td,sde->ste', h_one, w_qkv, precision=HIGHEST)
    queries = low(low_back(projected[0] + b_qv[0]))
    key_rows = low(low_back(projected[1]))
    values = low(low_back(projected[2] + b_qv[1]))
    attended = lax.map(jax.checkpoint(partial(head_attend, allowed)), (split_heads(queries), split_heads(key_rows), split_heads(values)))
    att_low = low(low_back(attended.transpose(1, 0, 2).reshape(PACK_LEN, D)))
    middle = rows_in + low_back(jnp.dot(att_low, w_out, precision=HIGHEST)) + b_out
    h_two = low(norm_rows(middle, gain_two, shift_two))
    pre_act = low_back(jnp.dot(h_two, w_fc, precision=HIGHEST) + b_fc)
    active = low(jax.nn.gelu(pre_act, approximate=True))
    return middle + low_back(jnp.dot(active, w_proj, precision=HIGHEST)) + b_proj

def reference(inputs, lengths, w_qkv, b_qv, w_out, b_out, w_fc, b_fc, w_proj, b_proj, gain_one, shift_one, gain_two, shift_two, cotangent):
    params = tuple((weight.astype(jnp.float32) for weight in (w_qkv, b_qv, w_out, b_out, w_fc, b_fc, w_proj, b_proj, gain_one, shift_one, gain_two, shift_two)))
    stacked_in = inputs.reshape(PACKS * N_DP, PACK_LEN, D)
    stacked_cot = cotangent.reshape(PACKS * N_DP, PACK_LEN, D)
    pack_lens = lengths.transpose(1, 0, 2).reshape(PACKS * N_DP, SEQS)
    initial = tuple((jnp.zeros(weight.shape, jnp.float32) for weight in params))
    places = jnp.arange(PACK_LEN, dtype=jnp.int32)

    def one_pack(totals, item):
        pack_in, pack_cot, pack_lengths = item
        doc_of = doc_ids(pack_lengths)
        allowed = (places[None, :] <= places[:, None]) & (doc_of[:, None] == doc_of[None, :])

        def forward(params_in, rows_in):
            return whole_layer(params_in, rows_in, allowed)
        result, pullback = jax.vjp(forward, params, pack_in.astype(jnp.float32))
        grad_params, grad_in = pullback(pack_cot.astype(jnp.float32))
        totals = jax.tree.map(lambda running, latest: running + latest, totals, grad_params)
        return (totals, (result.astype(jnp.bfloat16), grad_in))
    totals, (results, grads_in) = lax.scan(one_pack, initial, (stacked_in, stacked_cot, pack_lens))
    output = results.reshape(PACKS, N_DP * PACK_LEN, D)
    grad_inputs = grads_in.reshape(PACKS, N_DP * PACK_LEN, D)
    return (output, grad_inputs, totals[0], totals[1], totals[2], totals[3], totals[4], totals[5], totals[6], totals[7], totals[8], totals[9], totals[10], totals[11])
```

```python
import jax
import jax.numpy as jnp
from jax import lax
from jax.sharding import PartitionSpec as P

HEAD_DIM = 64
EPSILON = 1e-05
MASKED = -1000000000.0
BF = jnp.bfloat16
F32 = jnp.float32


def norm_parts(row_vals):
    row_mean = jnp.mean(row_vals, axis=-1, keepdims=True)
    centred = row_vals - row_mean
    inverse = lax.rsqrt(jnp.mean(centred * centred, axis=-1, keepdims=True) + EPSILON)
    return (centred * inverse, inverse)


def norm_back(grad_normed, normed, inverse):
    first_mean = jnp.mean(grad_normed, axis=-1, keepdims=True)
    second_mean = jnp.mean(grad_normed * normed, axis=-1, keepdims=True)
    return inverse * (grad_normed - first_mean - normed * second_mean)


def doc_ids(pack_lengths, pack_len):
    seq_count = pack_lengths.shape[0]
    seq_ends = jnp.cumsum(pack_lengths, dtype=jnp.int32)
    places = jnp.arange(pack_len, dtype=jnp.int32)
    passed = jnp.sum(
        (places[:, None] >= seq_ends[None, :]).astype(jnp.int32), axis=1, dtype=jnp.int32
    )
    return jnp.where(passed < seq_count, passed, seq_count + places)


def allowed_block(doc_of, first_row, block_rows):
    finish = first_row + block_rows
    query_pos = jnp.arange(first_row, finish)
    key_pos = jnp.arange(finish)
    causal = key_pos[None, :] <= query_pos[:, None]
    return causal & (doc_of[first_row:finish, None] == doc_of[None, :finish])


def block_scores(query_block, key_rows, doc_of, first_row, block_rows, scale):
    finish = first_row + block_rows
    scores = (
        jnp.einsum("qhe,khe->hqk", query_block, key_rows[:finish], preferred_element_type=F32)
        * scale
    )
    return jnp.where(allowed_block(doc_of, first_row, block_rows)[None], scores, MASKED)


def attend_forward(queries, key_rows, values, doc_of, block_rows, scale):
    outputs, log_sums = ([], [])
    for first_row in range(0, queries.shape[0], block_rows):
        finish = first_row + block_rows
        scores = block_scores(
            queries[first_row:finish], key_rows, doc_of, first_row, block_rows, scale
        )
        row_max = jnp.max(scores, axis=-1, keepdims=True)
        exponent = jnp.exp(scores - row_max)
        row_total = jnp.sum(exponent, axis=-1, keepdims=True)
        attn_probs = (exponent / row_total).astype(BF)
        outputs.append(
            jnp.einsum("hqk,khe->qhe", attn_probs, values[:finish], preferred_element_type=F32)
        )
        log_sums.append(row_max + jnp.log(row_total))
    return (jnp.concatenate(outputs, axis=0), log_sums)


def attend_backward(queries, key_rows, values, grad_att, doc_of, log_sums, block_rows, scale):
    grad_queries = []
    grad_keys = jnp.zeros(key_rows.shape, F32)
    grad_values = jnp.zeros(values.shape, F32)
    for block_num, first_row in enumerate(range(0, queries.shape[0], block_rows)):
        finish = first_row + block_rows
        query_block = queries[first_row:finish]
        grad_block = grad_att[first_row:finish]
        scores = block_scores(query_block, key_rows, doc_of, first_row, block_rows, scale)
        attn_probs = jnp.exp(scores - log_sums[block_num])
        grad_probs = jnp.einsum(
            "qhe,khe->hqk", grad_block, values[:finish], preferred_element_type=F32
        )
        row_delta = jnp.sum(attn_probs * grad_probs, axis=-1, keepdims=True)
        grad_scores = (attn_probs * (grad_probs - row_delta)).astype(BF)
        grad_queries.append(
            scale
            * jnp.einsum(
                "hqk,khe->qhe", grad_scores, key_rows[:finish], preferred_element_type=F32
            )
        )
        grad_keys = grad_keys.at[:finish].add(
            scale
            * jnp.einsum("hqk,qhe->khe", grad_scores, query_block, preferred_element_type=F32)
        )
        grad_values = grad_values.at[:finish].add(
            jnp.einsum(
                "hqk,qhe->khe", attn_probs.astype(BF), grad_block, preferred_element_type=F32
            )
        )
    return (jnp.concatenate(grad_queries, axis=0), grad_keys, grad_values)


def dp_bits():
    return (lax.axis_size("dp") - 1).bit_length()


def doubles():
    size = lax.axis_size("dp")
    return size == 1 << dp_bits() and 1 < size <= 8


def relative_blocks():
    size = lax.axis_size("dp")
    pos = jnp.arange(size, dtype=jnp.int32)
    if not doubles():
        return pos
    high = dp_bits() - 1
    return ((pos & ((1 << high) - 1)) << 1 | pos >> high) ^ lax.axis_index("dp")


def chosen_columns(width):
    each = width // lax.axis_size("dp")
    source = (relative_blocks()[:, None] * each + jnp.arange(each, dtype=jnp.int32)).reshape(-1)
    return (jnp.arange(width, dtype=jnp.int32)[:, None] == source[None, :]).astype(BF)


def flip(value, axis, bit):
    size = lax.axis_size(axis)
    return lax.ppermute(value, axis, [(i, i ^ (1 << bit)) for i in range(size)])


def after(value, other):
    return lax.optimization_barrier((value, other))[0]


def line_steps(block):
    size = lax.axis_size("tensor")
    from_low, from_high = [], []
    going_up = going_down = block
    for step in range(size - 1):
        going_up = lax.ppermute(going_up, "tensor", [(i, i + 1) for i in range(step, size - 1)])
        going_down = lax.ppermute(
            going_down, "tensor", [(i + 1, i) for i in range(size - 1 - step)]
        )
        from_low.append(going_up)
        from_high.append(going_down)
    return from_low, from_high


def line_order(block, from_low, from_high):
    size = lax.axis_size("tensor")
    stacked = jnp.stack(from_low[::-1] + [block] + from_high)
    return lax.dynamic_slice_in_dim(stacked, size - 1 - lax.axis_index("tensor"), size, 0)


def line_sum(term):
    size = lax.axis_size("tensor")
    place = lax.axis_index("tensor")
    up = down = None
    for step in range(1, size):
        part_up = term(jnp.minimum(place + size - step, size - 1))
        part_down = term(jnp.maximum(place - size + step, 0))
        if up is not None:
            part_up = part_up + up.astype(F32)
            part_down = part_down + down.astype(F32)
        up = lax.ppermute(part_up.astype(BF), "tensor", [(i, i + 1) for i in range(step)])
        down = lax.ppermute(
            part_down.astype(BF), "tensor", [(size - 1 - i, size - 2 - i) for i in range(step)]
        )
    return term(place) + up.astype(F32) + down.astype(F32)


def exchange(blocks):
    size = lax.axis_size("tensor")
    place = lax.axis_index("tensor")
    result = jnp.zeros_like(blocks)
    own = lax.dynamic_index_in_dim(blocks, place, 0)
    result = lax.dynamic_update_slice_in_dim(result, own, place, 0)
    for shift in range(1, size):
        sent = lax.dynamic_index_in_dim(blocks, (place + shift) % size, 0)
        came = lax.ppermute(sent, "tensor", [(i, (i + shift) % size) for i in range(size)])
        result = lax.dynamic_update_slice_in_dim(result, came, (place - shift) % size, 0)
    return result


def doubled(block, upward):
    if not doubles():
        return lax.all_gather(block, "dp", axis=1)
    high = list(range(1, dp_bits()))
    shape = block.shape
    held = []
    for bit in high if upward else high[::-1]:
        came = flip(block, "dp", bit)
        at = 1 + sum(b > bit for b in held)
        block = jnp.stack([block, came], axis=at)
        held.append(bit)
    block = jnp.stack([block, flip(block, "dp", 0)], axis=1)
    return block.reshape(shape[0], lax.axis_size("dp"), *shape[1:])


def halved(parts, upward):
    if not doubles():
        return lax.psum_scatter(parts, "dp", scatter_dimension=1)
    bits = dp_bits()
    high = list(range(1, bits))
    parts = parts.reshape(parts.shape[0], *[2] * bits, *parts.shape[2:])
    axes = {0: 1, **{b: 1 + bits - b for b in high}}
    for bit in [0] + (high[::-1] if upward else high):
        at = axes[bit]
        keep = lax.index_in_dim(parts, 0, at, keepdims=False)
        came = flip(lax.index_in_dim(parts, 1, at, keepdims=False), "dp", bit)
        parts = (keep.astype(F32) + came.astype(F32)).astype(BF)
        axes = {b: a - (a > at) for b, a in axes.items()}
    return parts


def total(vector, axis):
    for bit in range((lax.axis_size(axis) - 1).bit_length()):
        vector = vector + flip(vector, axis, bit)
    return vector


def on_device(
    inputs,
    lengths,
    w_qkv,
    b_qv,
    w_out,
    b_out,
    w_fc,
    b_fc,
    w_proj,
    b_proj,
    gain_one,
    shift_one,
    gain_two,
    shift_two,
    cotangent,
):
    row_count, model_width = inputs.shape[1:]
    tensor_size = lax.axis_size("tensor")
    dp_size = lax.axis_size("dp")
    tensor_pos = lax.axis_index("tensor")
    pack_len = row_count * tensor_size
    head_width = w_qkv.shape[2]
    local_heads = head_width // HEAD_DIM
    block_rows = min(512, pack_len)
    scale = HEAD_DIM ** (-0.5)
    fc_local = b_fc.shape[0]
    owned = model_width // dp_size
    out_rows = owned * head_width // fc_local
    place = chosen_columns(model_width)

    def relative(rows):
        return jnp.dot(rows, place, preferred_element_type=F32)

    def absolute(rows):
        return jnp.einsum(
            "td,cd->tc",
            rows,
            place.astype(rows.dtype),
            precision=lax.Precision.HIGHEST,
            preferred_element_type=F32,
        )

    shard = jnp.concatenate([w_fc, w_proj.T, w_out.T.reshape(out_rows, fc_local), b_fc[None]])
    shard_low, shard_high = line_steps(shard)
    qkv_rows = jnp.concatenate([w_qkv[0], w_qkv[1], w_qkv[2]], axis=1)
    qkv_full = doubled(qkv_rows[None], True).reshape(model_width, 3 * head_width)

    vectors = relative(jnp.stack([gain_one, shift_one, gain_two, shift_two, b_out, b_proj]))
    gain_first, shift_first, gain_second, shift_second, bias_out, bias_proj = vectors
    rows_in = relative(inputs[0])
    normed_one, inverse_one = norm_parts(rows_in)
    h_one = (normed_one * gain_first + shift_first).astype(BF)
    h_one = after(h_one, (shard_low[-2], shard_high[-2]))
    h_one_all = line_order(h_one, *line_steps(h_one)).reshape(pack_len, model_width)

    shards = line_order(shard, shard_low, shard_high)
    cut = 2 * owned
    bias_fc = shards[:, -1:].astype(F32)
    some_out = jnp.concatenate([shards[:, :owned], shards[:, cut:-1]], axis=1)
    half_a = doubled(some_out, True)
    half_b = doubled(shards[:, owned:cut], False)
    fc_full = half_a[:, :, :owned].reshape(tensor_size, model_width, fc_local)
    out_t = half_a[:, :, owned:].reshape(tensor_size, model_width, head_width)
    proj_t = half_b.reshape(tensor_size, model_width, fc_local)

    doc_of = doc_ids(lengths[0, 0], pack_len)
    projected = jnp.dot(h_one_all, qkv_full, preferred_element_type=F32)
    projected = projected.reshape(pack_len, 3, local_heads, HEAD_DIM)
    bias_qv = b_qv.astype(F32).reshape(2, local_heads, HEAD_DIM)
    queries = (projected[:, 0] + bias_qv[0]).astype(BF)
    key_rows = projected[:, 1].astype(BF)
    values = (projected[:, 2] + bias_qv[1]).astype(BF)
    attended, log_sums = attend_forward(queries, key_rows, values, doc_of, block_rows, scale)
    att = exchange(attended.astype(BF).reshape(tensor_size, row_count, head_width))

    middle = (
        rows_in + jnp.einsum("ztc,zdc->td", att, out_t, preferred_element_type=F32) + bias_out
    )
    normed_two, inverse_two = norm_parts(middle)
    h_two = (normed_two * gain_second + shift_second).astype(BF)
    pre_act = jnp.einsum("td,zdf->ztf", h_two, fc_full, preferred_element_type=F32) + bias_fc
    root = (2.0 / jnp.pi) ** 0.5
    bend = jnp.tanh(root * (pre_act + 0.044715 * pre_act * pre_act * pre_act))
    active = (0.5 * pre_act * (1.0 + bend)).astype(BF)
    slope = 0.5 * (1.0 + bend) + 0.5 * pre_act * (1.0 - bend * bend) * root * (
        1.0 + 3 * 0.044715 * pre_act * pre_act
    )
    mlp_out = jnp.einsum("ztf,zdf->td", active, proj_t, preferred_element_type=F32)
    output = absolute((middle + mlp_out + bias_proj).astype(BF)).astype(BF)

    grad_y = relative(cotangent[0])
    grad_low = grad_y.astype(BF)
    grad_active = jnp.einsum("td,zdf->ztf", grad_low, proj_t, preferred_element_type=F32)
    grad_pre = (grad_active * slope).astype(BF)
    grad_h_two = jnp.einsum("ztf,zdf->td", grad_pre, fc_full, preferred_element_type=F32)
    grad_middle = grad_y + norm_back(grad_h_two * gain_second, normed_two, inverse_two)
    grad_branch = grad_middle.astype(BF)
    grad_att_rows = jnp.einsum("td,zdc->ztc", grad_branch, out_t, preferred_element_type=F32)
    heads_shape = (pack_len, local_heads, HEAD_DIM)
    grad_att = exchange(grad_att_rows.astype(BF)).reshape(heads_shape)

    def by_owner(left, right):
        full = jnp.einsum("td,ztf->zdf", left, right, preferred_element_type=F32).astype(BF)
        return full.reshape(tensor_size, dp_size, owned, right.shape[2])

    d_proj_all = by_owner(grad_low, active)
    d_fc_all = by_owner(h_two, grad_pre)
    d_out_all = by_owner(grad_branch, att).reshape(tensor_size, dp_size, out_rows, fc_local)
    part_a = halved(jnp.concatenate([d_fc_all, d_out_all], axis=2), True)
    part_b = halved(d_proj_all, False)
    shard_part = jnp.concatenate([part_a, part_b], axis=1)
    d_shard = line_sum(lambda j: lax.dynamic_index_in_dim(shard_part, j, 0, keepdims=False))
    d_fc = d_shard[:owned]
    d_out = d_shard[owned : owned + out_rows].reshape(owned, head_width).T
    d_proj = d_shard[owned + out_rows :].T

    early_rows = jnp.stack(
        [
            jnp.sum(grad_h_two * normed_two, axis=0),
            jnp.sum(grad_h_two, axis=0),
            jnp.sum(grad_middle, axis=0),
            jnp.sum(grad_y, axis=0),
        ]
    )
    early_fc = jnp.sum(grad_pre, axis=1, dtype=F32).reshape(-1)
    early = total(
        total(jnp.concatenate([absolute(early_rows).reshape(-1), early_fc]), "dp"), "tensor"
    )

    grad_query, grad_key, grad_value = attend_backward(
        queries, key_rows, values, grad_att, doc_of, log_sums, block_rows, scale
    )
    stacked = jnp.concatenate(
        [g.reshape(pack_len, head_width) for g in (grad_query, grad_key, grad_value)], axis=1
    ).astype(BF)
    sums = jnp.sum(stacked, axis=0, dtype=F32)
    sum_qv = jnp.stack([sums[:head_width], sums[2 * head_width :]])

    def input_term(j):
        mine = lax.dynamic_slice_in_dim(stacked, j * row_count, row_count, 0)
        return jnp.einsum("te,de->td", mine, qkv_full, preferred_element_type=F32)

    grad_h_one = line_sum(input_term)
    qkv_all = jnp.einsum("td,te->de", h_one_all, stacked, preferred_element_type=F32).astype(BF)
    d_qkv = halved(qkv_all.reshape(1, dp_size, owned, 3 * head_width), True)[0]
    d_qkv = d_qkv.astype(F32).reshape(owned, 3, head_width).transpose(1, 0, 2)

    grad_in = absolute(
        grad_middle + norm_back(grad_h_one * gain_first, normed_one, inverse_one)
    )
    late_rows = jnp.stack([jnp.sum(grad_h_one * normed_one, axis=0), jnp.sum(grad_h_one, axis=0)])
    late = total(
        jnp.concatenate([absolute(late_rows).reshape(-1), sum_qv.reshape(-1)]), "dp"
    )
    wide = model_width
    sum_qv = late[2 * wide :].reshape(2, head_width)
    late = total(late[: 2 * wide], "tensor")
    d_b_fc = lax.dynamic_slice(early[4 * wide :], (tensor_pos * fc_local,), (fc_local,))
    return (
        output[None],
        grad_in[None],
        d_qkv,
        sum_qv,
        d_out,
        early[2 * wide : 3 * wide],
        d_fc,
        d_b_fc,
        d_proj,
        early[3 * wide : 4 * wide],
        late[:wide],
        late[wide:],
        early[:wide],
        early[wide : 2 * wide],
    )


def solution(mesh):
    rows = P(None, ("dp", "tensor"), None)
    placed = (
        rows,
        P("dp", None, None),
        P(None, "dp", "tensor"),
        P(None, "tensor"),
        P("tensor", "dp"),
        P(),
        P("dp", "tensor"),
        P("tensor"),
        P("tensor", "dp"),
        P(),
        P(),
        P(),
        P(),
        P(),
        rows,
    )
    return jax.shard_map(
        on_device,
        mesh=mesh,
        in_specs=placed,
        out_specs=(
            rows,
            rows,
            P(None, "dp", "tensor"),
            P(None, "tensor"),
            P("tensor", "dp"),
            P(),
            P("dp", "tensor"),
            P("tensor"),
            P("tensor", "dp"),
            P(),
            P(),
            P(),
            P(),
            P(),
        ),
        check_vma=False,
    )
```

```python
from functools import partial

import jax
import jax.numpy as jnp
from jax import lax
from jax.experimental import pallas as pl
from jax.experimental.pallas import tpu as pltpu
from jax.sharding import PartitionSpec as P

HEAD_DIM = 64
EPSILON = 1e-05
MASKED = -1000000000.0
BF = jnp.bfloat16
F32 = jnp.float32


def norm_parts(row_vals):
    row_mean = jnp.mean(row_vals, axis=-1, keepdims=True)
    centred = row_vals - row_mean
    inverse = lax.rsqrt(jnp.mean(centred * centred, axis=-1, keepdims=True) + EPSILON)
    return (centred * inverse, inverse)


def norm_back(grad_normed, normed, inverse):
    first_mean = jnp.mean(grad_normed, axis=-1, keepdims=True)
    second_mean = jnp.mean(grad_normed * normed, axis=-1, keepdims=True)
    return inverse * (grad_normed - first_mean - normed * second_mean)


def first_allowed(pack_lengths, pack_len):
    seq_ends = jnp.cumsum(pack_lengths, dtype=jnp.int32)
    seq_starts = seq_ends - pack_lengths
    places = jnp.arange(pack_len, dtype=jnp.int32)[None, :]
    inside = (places >= seq_starts[:, None]) & (places < seq_ends[:, None])
    started = jnp.max(jnp.where(inside, seq_starts[:, None], -1), axis=0, keepdims=True)
    return jnp.where(started >= 0, started, places)


def contract(left, right, left_dim, right_dim):
    return lax.dot_general(
        left, right, (((left_dim,), (right_dim,)), ((), ())), preferred_element_type=F32
    )


def join(parts):
    return parts[0] if len(parts) == 1 else jnp.concatenate(parts, axis=0)


def masked(scores, first, row):
    keys, queries = scores.shape
    parts = []
    if row:
        key_pos = lax.broadcasted_iota(jnp.int32, (row, queries), 0)
        parts.append(jnp.where(key_pos >= first, scores[:row], MASKED))
    key_pos = row + lax.broadcasted_iota(jnp.int32, (keys - row, queries), 0)
    query_pos = row + lax.broadcasted_iota(jnp.int32, (1, queries), 1)
    ok = (key_pos >= first) & (key_pos <= query_pos)
    parts.append(jnp.where(ok, scores[row:], MASKED))
    return parts


def query_block(rows):
    return min(256, rows)


def relative_block(place_ref, block, blocks):
    return lax.rem(block - place_ref[0] + blocks, blocks)


def forward_kernel(place_ref, qkv_ref, first_ref, att_ref, lse_ref, values_ref):
    blocks, each_rows = att_ref.shape[:2]
    rows = blocks * each_rows
    each = 3 * HEAD_DIM
    heads = qkv_ref.shape[1] // each
    block = query_block(each_rows)
    scale = jnp.asarray(HEAD_DIM**-0.5, BF)
    for row in range(0, rows, block):
        vals = [
            qkv_ref[row : row + block, (h + 1) * each - HEAD_DIM : (h + 1) * each]
            for h in range(heads)
        ]
        values_ref[:, row : row + block] = jnp.concatenate(vals, axis=1).astype(F32).T.astype(BF)
    for row in range(0, rows, block):
        end = row + block
        first = first_ref[:, row:end]
        outs = []
        for h in range(heads):
            c = h * each
            queries = qkv_ref[row:end, c : c + HEAD_DIM] * scale
            keys = qkv_ref[:end, c + HEAD_DIM : c + 2 * HEAD_DIM]
            scores = masked(contract(keys, queries, 1, 1), first, row)
            peak = jnp.max(scores[-1], axis=0, keepdims=True)
            if row:
                peak = jnp.maximum(peak, jnp.max(scores[0], axis=0, keepdims=True))
            exponents = [jnp.exp(part - peak) for part in scores]
            sums = sum(jnp.sum(part, axis=0, keepdims=True) for part in exponents)
            values = values_ref[h * HEAD_DIM : (h + 1) * HEAD_DIM, :end]
            low = join([part.astype(BF) for part in exponents])
            outs.append(contract(values, low, 1, 0) / sums)
            lse_ref[h : h + 1, row:end] = peak + jnp.log(sums)
        d = relative_block(place_ref, row // each_rows, blocks)
        at = row % each_rows
        att_ref[d, at : at + block, :] = jnp.concatenate(outs, axis=0).T.astype(BF)


def backward_kernel(head, place_ref, qkv_ref, att_ref, lse_ref, first_ref, *refs):
    grads_in, (out_ref, keys_ref, sum_ref, grad_ref) = refs[:-4], refs[-4:]
    blocks, each_rows = att_ref.shape[:2]
    rows = blocks * each_rows
    block = query_block(each_rows)
    scale = jnp.asarray(HEAD_DIM**-0.5, BF)
    c = head * 3 * HEAD_DIM
    e = head * HEAD_DIM
    for d, block_ref in enumerate(grads_in):
        grad_ref[d] = block_ref[:, e : e + HEAD_DIM]
    for row in range(0, rows, block):
        keys = qkv_ref[row : row + block, c + HEAD_DIM : c + 2 * HEAD_DIM] * scale
        keys_ref[:, row : row + block] = keys.astype(F32).T.astype(BF)
    sum_ref[...] = jnp.zeros_like(sum_ref)
    zero = jnp.zeros((block, HEAD_DIM), BF)
    for row in range(rows - block, -1, -block):
        end = row + block
        d = relative_block(place_ref, row // each_rows, blocks)
        at = row % each_rows
        queries = qkv_ref[row:end, c : c + HEAD_DIM] * scale
        keys = qkv_ref[:end, c + HEAD_DIM : c + 2 * HEAD_DIM]
        values = qkv_ref[:end, c + 2 * HEAD_DIM : c + 3 * HEAD_DIM]
        grad = grad_ref[d, at : at + block, :]
        att = att_ref[d, at : at + block, e : e + HEAD_DIM]
        delta = jnp.sum((grad.astype(F32) * att.astype(F32)).T, axis=0, keepdims=True)
        scores = masked(contract(keys, queries, 1, 1), first_ref[:, row:end], row)
        lse = lse_ref[head : head + 1, row:end]
        probs = join([jnp.exp(part - lse) for part in scores])
        grad_scores = (probs * (contract(values, grad, 1, 1) - delta)).astype(BF)
        grad_queries = contract(keys_ref[:, :end], grad_scores, 1, 0)
        out_ref[row:end, :HEAD_DIM] = grad_queries.T.astype(BF)
        right = jnp.concatenate(
            [
                jnp.concatenate([queries, zero], axis=1),
                jnp.concatenate([zero, grad], axis=1),
            ],
            axis=0,
        )
        left = jnp.concatenate([grad_scores, probs.astype(BF)], axis=1)
        sum_ref[:end, :] += jnp.dot(left, right, preferred_element_type=F32)
    out_ref[:, HEAD_DIM:] = sum_ref[...].astype(BF)


def kernel_call(kernel, out_shape, scratch_shapes, flops, place, *args):
    whole = pl.BlockSpec(memory_space=pltpu.VMEM)
    return pl.pallas_call(
        kernel,
        out_shape=out_shape,
        in_specs=[pl.BlockSpec(memory_space=pltpu.SMEM)] + [whole] * len(args),
        out_specs=jax.tree.map(lambda _: whole, out_shape),
        scratch_shapes=scratch_shapes,
        compiler_params=pltpu.CompilerParams(vmem_limit_bytes=48 * 2**20),
        cost_estimate=pl.CostEstimate(
            flops=flops, bytes_accessed=sum(a.size * 2 for a in args), transcendentals=flops // 64
        ),
    )(place, *args)


def attend_forward(place, qkv, first, blocks):
    rows, width = qkv.shape
    shapes = (
        jax.ShapeDtypeStruct((blocks, rows // blocks, width // 3), BF),
        jax.ShapeDtypeStruct((8 * pl.cdiv(width // (3 * HEAD_DIM), 8), rows), F32),
    )
    scratch = [pltpu.VMEM((width // 3, rows), BF)]
    flops = 8 * rows * rows * width // 3
    return kernel_call(forward_kernel, shapes, scratch, flops, place, qkv, first)


def attend_backward(head, place, qkv, att, lse, first, grads):
    blocks, each_rows = att.shape[:2]
    rows = qkv.shape[0]
    shape = jax.ShapeDtypeStruct((rows, 3 * HEAD_DIM), BF)
    scratch = [
        pltpu.VMEM((HEAD_DIM, rows), BF),
        pltpu.VMEM((rows, 2 * HEAD_DIM), F32),
        pltpu.VMEM((blocks, each_rows, HEAD_DIM), BF),
    ]
    flops = 2 * rows * rows * HEAD_DIM
    kernel = partial(backward_kernel, head)
    return kernel_call(kernel, shape, scratch, flops, place, qkv, att, lse, first, *grads)


def dp_bits():
    return (lax.axis_size("dp") - 1).bit_length()


def doubles():
    size = lax.axis_size("dp")
    return size == 1 << dp_bits() and 1 < size <= 8


def relative_blocks():
    size = lax.axis_size("dp")
    pos = jnp.arange(size, dtype=jnp.int32)
    if not doubles():
        return pos
    high = dp_bits() - 1
    return ((pos & ((1 << high) - 1)) << 1 | pos >> high) ^ lax.axis_index("dp")


def chosen_columns(width):
    each = width // lax.axis_size("dp")
    source = (relative_blocks()[:, None] * each + jnp.arange(each, dtype=jnp.int32)).reshape(-1)
    return (jnp.arange(width, dtype=jnp.int32)[:, None] == source[None, :]).astype(BF)


def flip(value, axis, bit):
    size = lax.axis_size(axis)
    return lax.ppermute(value, axis, [(i, i ^ (1 << bit)) for i in range(size)])


def after(value, other):
    return lax.optimization_barrier((value, other))[0]


def exchange(blocks):
    size = lax.axis_size("tensor")
    came = [
        lax.ppermute(blocks[d], "tensor", [(i, (i + d) % size) for i in range(size)])
        for d in range(1, size)
    ]
    return [blocks[0]] + came[::-1]


def fold(rows, width):
    groups = width // rows.shape[-1]
    each = rows.shape[-2] // groups
    return jnp.concatenate(
        [rows[..., g * each : (g + 1) * each, :] for g in range(groups)], axis=-1
    )


def unfold(rows, width):
    groups = rows.shape[-1] // width
    return jnp.concatenate([rows[..., g * width : (g + 1) * width] for g in range(groups)], axis=-2)


class Doubling:
    def __init__(self, block, upward):
        high = list(range(1, dp_bits()))
        self.block, self.shape, self.held, self.came = block, block.shape, [], None
        self.bits = (high if upward else high[::-1]) + [0] if doubles() else []

    def start(self):
        self.came = flip(self.block, "dp", self.bits[0]) if self.bits else self.block

    def step(self):
        if self.bits:
            bit = self.bits.pop(0)
            at = 1 + sum(b > bit for b in self.held) if bit else 1
            came = flip(self.block, "dp", bit) if self.came is None else self.came
            self.came = None
            self.block = jnp.stack([self.block, came], axis=at)
            self.held.append(bit)

    def result(self):
        while self.bits:
            self.step()
        if not self.held:
            return lax.all_gather(self.block, "dp", axis=1)
        return self.block.reshape(self.shape[0], lax.axis_size("dp"), *self.shape[1:])


class Halving:
    def __init__(self, parts, upward):
        bits = dp_bits()
        high = list(range(1, bits))
        self.block, self.bits, self.axes = parts, [], None
        if doubles():
            self.block = parts.reshape(parts.shape[0], *[2] * bits, *parts.shape[2:])
            self.bits = [0] + (high[::-1] if upward else high)
            self.axes = {0: 1, **{b: 1 + bits - b for b in high}}

    def step(self):
        if self.bits:
            bit = self.bits.pop(0)
            at = self.axes[bit]
            keep = lax.index_in_dim(self.block, 0, at, keepdims=False)
            came = flip(lax.index_in_dim(self.block, 1, at, keepdims=False), "dp", bit)
            self.block = (keep.astype(F32) + came.astype(F32)).astype(BF)
            self.axes = {b: a - (a > at) for b, a in self.axes.items()}

    def result(self):
        if self.axes is None:
            return lax.psum_scatter(self.block, "dp", scatter_dimension=1)
        while self.bits:
            self.step()
        return self.block


def total(vector, axis):
    for bit in range((lax.axis_size(axis) - 1).bit_length()):
        vector = vector + flip(vector, axis, bit)
    return vector


def on_device(
    inputs,
    lengths,
    w_qkv,
    b_qv,
    w_out,
    b_out,
    w_fc,
    b_fc,
    w_proj,
    b_proj,
    gain_one,
    shift_one,
    gain_two,
    shift_two,
    cotangent,
):
    row_count, model_width = inputs.shape[1:]
    tensor_size = lax.axis_size("tensor")
    dp_size = lax.axis_size("dp")
    tensor_pos = lax.axis_index("tensor")
    pack_len = row_count * tensor_size
    head_width = w_qkv.shape[2]
    local_heads = head_width // HEAD_DIM
    fc_local = b_fc.shape[0]
    owned = model_width // dp_size
    out_rows = owned * head_width // fc_local
    place = chosen_columns(model_width)

    def relative(rows):
        return jnp.dot(rows, place, preferred_element_type=F32)

    def absolute(rows):
        return jnp.einsum(
            "td,cd->tc",
            rows,
            place.astype(rows.dtype),
            precision=lax.Precision.HIGHEST,
            preferred_element_type=F32,
        )

    qkv_rows = w_qkv.reshape(3, owned, local_heads, HEAD_DIM).transpose(1, 2, 0, 3)
    qkv_full = Doubling(qkv_rows.reshape(1, owned, 3 * head_width), True).result()
    vectors = relative(jnp.stack([gain_one, shift_one, gain_two, shift_two, b_out, b_proj]))
    gain_first, shift_first, gain_second, shift_second, bias_out, bias_proj = vectors
    rows_in = relative(inputs[0])
    normed_one, _ = norm_parts(rows_in)
    h_one = (normed_one * gain_first + shift_first).astype(BF)
    h_one_all = lax.all_gather(h_one, "tensor", axis=0, tiled=True)

    shard = jnp.concatenate([w_fc, w_proj.T, fold(w_out.T, fc_local), b_fc[None]])
    shards = exchange([shard] * tensor_size)
    shards, qkv_full = lax.optimization_barrier((shards, qkv_full))
    qkv_full = qkv_full.reshape(model_width, 3 * head_width)

    bias_fc = jnp.stack([part[-1:] for part in shards]).astype(F32)
    outs = [unfold(part[2 * owned : -1], head_width) for part in shards]
    gathers = [
        Doubling(jnp.stack([part[:owned] for part in shards]), True),
        Doubling(jnp.stack([part[owned : 2 * owned] for part in shards]), False),
        Doubling(jnp.concatenate(outs, axis=1)[None], True),
    ]
    for gather in gathers:
        gather.step()
    held = lax.optimization_barrier([g.block for g in gathers])
    for gather, block in zip(gathers, held):
        gather.block = block

    place_on_line = tensor_pos.astype(jnp.int32).reshape(1)
    first = first_allowed(lengths[0, 0], pack_len)
    none = jnp.zeros_like(b_qv[0])
    bias_qkv = jnp.stack([b_qv[0], none, b_qv[1]]).astype(F32)
    bias_qkv = bias_qkv.reshape(3, local_heads, HEAD_DIM).transpose(1, 0, 2).reshape(-1)
    projected = jnp.dot(h_one_all, qkv_full, preferred_element_type=F32)
    qkv = (projected + bias_qkv).astype(BF)
    att_all, lse = attend_forward(place_on_line, qkv, first, tensor_size)
    for gather in gathers:
        gather.start()
    att_all, held = lax.optimization_barrier((att_all, [g.came for g in gathers]))
    for gather, came in zip(gathers, held):
        gather.came = came
        gather.step()
    att = exchange([att_all[d] for d in range(tensor_size)])
    att, held = lax.optimization_barrier((att, [g.block for g in gathers]))
    for gather, block in zip(gathers, held):
        gather.block = block
    att_rows = jnp.concatenate(att, axis=1)
    fc_full, proj_t, out_t = [gather.result() for gather in gathers]
    fc_full = fc_full.reshape(tensor_size, model_width, fc_local)
    proj_t = proj_t.reshape(tensor_size, model_width, fc_local)
    out_t = out_t.reshape(model_width, model_width)

    middle = (
        rows_in + jnp.einsum("tc,dc->td", att_rows, out_t, preferred_element_type=F32) + bias_out
    )
    normed_two, inverse_two = norm_parts(middle)
    h_two = (normed_two * gain_second + shift_second).astype(BF)
    pre_act = jnp.einsum("td,zdf->ztf", h_two, fc_full, preferred_element_type=F32) + bias_fc
    root = (2.0 / jnp.pi) ** 0.5
    bend = jnp.tanh(root * (pre_act + 0.044715 * pre_act * pre_act * pre_act))
    active = (0.5 * pre_act * (1.0 + bend)).astype(BF)
    slope = 0.5 * (1.0 + bend) + 0.5 * pre_act * (1.0 - bend * bend) * root * (
        1.0 + 3 * 0.044715 * pre_act * pre_act
    )
    grad_y = relative(cotangent[0])
    grad_low = grad_y.astype(BF)
    grad_active = jnp.einsum("td,zdf->ztf", grad_low, proj_t, preferred_element_type=F32)
    grad_pre = (grad_active * slope).astype(BF)
    grad_h_two = jnp.einsum("ztf,zdf->td", grad_pre, fc_full, preferred_element_type=F32)
    grad_middle = grad_y + norm_back(grad_h_two * gain_second, normed_two, inverse_two)
    grad_branch = grad_middle.astype(BF)
    grad_att_rows = jnp.dot(grad_branch, out_t, preferred_element_type=F32).astype(BF)
    grad_att = exchange(
        [grad_att_rows[:, d * head_width : (d + 1) * head_width] for d in range(tensor_size)]
    )


    def by_owner(left, right):
        full = jnp.einsum("td,ztf->zdf", left, right, preferred_element_type=F32).astype(BF)
        return full.reshape(tensor_size, dp_size, owned, fc_local)

    d_out_all = jnp.einsum(
        "td,tc->dc", grad_branch, att_rows, preferred_element_type=F32
    )
    parts = [
        Halving(by_owner(h_two, grad_pre), True),
        Halving(by_owner(grad_low, active), False),
        Halving(d_out_all.astype(BF).reshape(1, dp_size, owned, model_width), True),
    ]
    for part in parts:
        part.step()

    early_rows = jnp.stack(
        [
            jnp.sum(grad_h_two * normed_two, axis=0),
            jnp.sum(grad_h_two, axis=0),
            jnp.sum(grad_middle, axis=0),
            jnp.sum(grad_y, axis=0),
        ]
    )
    sums_fc = jnp.sum(grad_pre, axis=1, dtype=F32)

    by_head = []
    for head in range(local_heads):
        by_head.append(attend_backward(head, place_on_line, qkv, att_all, lse, first, grad_att))
        if head == 0:
            grad_att, held, by_head[0] = lax.optimization_barrier(
                (grad_att, [part.block for part in parts], by_head[0])
            )
            for part, block in zip(parts, held):
                part.block = block
                part.step()
    stacked = jnp.concatenate(by_head, axis=1)

    def tied(values):
        values, held = lax.optimization_barrier((values, [part.block for part in parts]))
        for part, block in zip(parts, held):
            part.block = block
        return values

    qkv_absolute = jnp.dot(place, qkv_full, preferred_element_type=F32).astype(BF)
    grad_middle = absolute(grad_middle)
    terms = jnp.einsum("te,ce->tc", stacked, qkv_absolute, preferred_element_type=F32).astype(BF)
    grad_h_one = lax.psum_scatter(terms, "tensor", scatter_dimension=0, tiled=True).astype(F32)
    stacked, grad_middle, terms = tied((stacked, grad_middle, terms))
    for part in parts:
        part.step()
    stacked = tied(stacked)
    mlp_out = jnp.einsum("ztf,zdf->td", after(active, terms), proj_t, preferred_element_type=F32)
    output = absolute((middle + mlp_out + bias_proj).astype(BF)).astype(BF)

    sums_fc_w, sums_proj_w, sums_out_w = [part.result() for part in parts]
    pieces = [
        jnp.concatenate(
            [
                sums_fc_w[d],
                sums_proj_w[d],
                fold(sums_out_w[0, :, d * head_width : (d + 1) * head_width], fc_local),
            ]
        )
        for d in range(tensor_size)
    ]
    pieces = exchange(pieces)
    d_shard = sum(came.astype(F32) for came in pieces)
    d_fc = d_shard[:owned]
    d_proj = d_shard[owned : 2 * owned].T
    d_out = unfold(d_shard[2 * owned :], head_width).T

    sums = jnp.sum(stacked, axis=0, dtype=F32)
    sums_by = sums.reshape(local_heads, 3, HEAD_DIM).transpose(1, 0, 2).reshape(3, head_width)
    sum_qv = sums_by[0::2]
    qkv_all = jnp.einsum(
        "td,te->de",
        h_one_all,
        stacked,
        preferred_element_type=F32,
    )
    wide_weights = qkv_full.astype(F32)
    normed_sums = (qkv_all - shift_first[:, None] * sums[None, :]) / gain_first[:, None]
    late_rows = jnp.stack(
        [
            jnp.sum(wide_weights * normed_sums, axis=1),
            jnp.sum(wide_weights * sums[None, :], axis=1),
        ]
    )
    d_qkv = Halving(qkv_all.astype(BF).reshape(1, dp_size, owned, 3 * head_width), True)
    d_qkv = d_qkv.result()[0]
    d_qkv = d_qkv.astype(F32).reshape(owned, local_heads, 3, HEAD_DIM).transpose(2, 0, 1, 3)
    d_qkv = d_qkv.reshape(3, owned, head_width)

    normed_rows, inverse_rows = norm_parts(inputs[0].astype(F32))
    grad_in = grad_middle + norm_back(
        grad_h_one * gain_one.astype(F32), normed_rows, inverse_rows
    )
    wide = model_width
    placed_fc = lax.dynamic_update_slice(
        jnp.zeros((2 * tensor_size, fc_local), F32), sums_fc, (tensor_pos, 0)
    )
    placed_fc = placed_fc[:tensor_size] + placed_fc[tensor_size:]
    rows = absolute(jnp.concatenate([early_rows, late_rows])).reshape(-1)
    sums_all = total(
        jnp.concatenate([rows, placed_fc.reshape(-1), sum_qv.reshape(-1)]), "dp"
    )
    sum_qv = sums_all[rows.size + placed_fc.size :].reshape(2, head_width)
    sums_all = after(sums_all[: rows.size + placed_fc.size], pieces)
    sums_all = total(sums_all, "tensor")
    d_gain_two, d_shift_two, d_b_out, d_b_proj, d_gain_one, d_shift_one = (
        sums_all[: 6 * wide].reshape(6, wide)
    )
    d_b_fc = lax.dynamic_slice(sums_all[6 * wide :], (tensor_pos * fc_local,), (fc_local,))
    return (
        output[None],
        grad_in[None],
        d_qkv,
        sum_qv,
        d_out,
        d_b_out,
        d_fc,
        d_b_fc,
        d_proj,
        d_b_proj,
        d_gain_one,
        d_shift_one,
        d_gain_two,
        d_shift_two,
    )


def solution(mesh):
    rows = P(None, ("dp", "tensor"), None)
    placed = (
        rows,
        P("dp", None, None),
        P(None, "dp", "tensor"),
        P(None, "tensor"),
        P("tensor", "dp"),
        P(),
        P("dp", "tensor"),
        P("tensor"),
        P("tensor", "dp"),
        P(),
        P(),
        P(),
        P(),
        P(),
        rows,
    )
    return jax.shard_map(
        on_device,
        mesh=mesh,
        in_specs=placed,
        out_specs=(
            rows,
            rows,
            P(None, "dp", "tensor"),
            P(None, "tensor"),
            P("tensor", "dp"),
            P(),
            P("dp", "tensor"),
            P("tensor"),
            P("tensor", "dp"),
            P(),
            P(),
            P(),
            P(),
            P(),
        ),
        check_vma=False,
    )
```

```python
from functools import partial

import jax
import jax.numpy as jnp
from jax import lax
from jax.experimental import pallas as pl
from jax.experimental.pallas import tpu as pltpu
from jax.sharding import PartitionSpec as P

HEAD_DIM = 64
EPSILON = 1e-05
MASKED = -1000000000.0
BF = jnp.bfloat16
F32 = jnp.float32


def norm_parts(row_vals):
    row_mean = jnp.mean(row_vals, axis=-1, keepdims=True)
    centred = row_vals - row_mean
    inverse = lax.rsqrt(jnp.mean(centred * centred, axis=-1, keepdims=True) + EPSILON)
    return (centred * inverse, inverse)


def norm_back(grad_normed, normed, inverse):
    first_mean = jnp.mean(grad_normed, axis=-1, keepdims=True)
    second_mean = jnp.mean(grad_normed * normed, axis=-1, keepdims=True)
    return inverse * (grad_normed - first_mean - normed * second_mean)


def first_allowed(pack_lengths, pack_len):
    seq_ends = jnp.cumsum(pack_lengths, dtype=jnp.int32)
    seq_starts = seq_ends - pack_lengths
    places = jnp.arange(pack_len, dtype=jnp.int32)[None, :]
    inside = (places >= seq_starts[:, None]) & (places < seq_ends[:, None])
    started = jnp.max(jnp.where(inside, seq_starts[:, None], -1), axis=0, keepdims=True)
    return jnp.where(started >= 0, started, places)


def contract(left, right, left_dim, right_dim):
    return lax.dot_general(
        left, right, (((left_dim,), (right_dim,)), ((), ())), preferred_element_type=F32
    )


def join(parts):
    return parts[0] if len(parts) == 1 else jnp.concatenate(parts, axis=0)


def masked(scores, first, row):
    keys, queries = scores.shape
    parts = []
    if row:
        key_pos = lax.broadcasted_iota(jnp.int32, (row, queries), 0)
        parts.append(jnp.where(key_pos >= first, scores[:row], MASKED))
    key_pos = row + lax.broadcasted_iota(jnp.int32, (keys - row, queries), 0)
    query_pos = row + lax.broadcasted_iota(jnp.int32, (1, queries), 1)
    ok = (key_pos >= first) & (key_pos <= query_pos)
    parts.append(jnp.where(ok, scores[row:], MASKED))
    return parts


def query_block(rows):
    return min(256, rows)


def relative_block(place_ref, block, blocks):
    return lax.rem(block - place_ref[0] + blocks, blocks)


def forward_kernel(place_ref, qkv_ref, first_ref, att_ref, lse_ref, values_ref):
    blocks, each_rows = att_ref.shape[:2]
    rows = blocks * each_rows
    each = 3 * HEAD_DIM
    heads = qkv_ref.shape[1] // each
    block = query_block(each_rows)
    scale = jnp.asarray(HEAD_DIM**-0.5, BF)
    for row in range(0, rows, block):
        vals = [
            qkv_ref[row : row + block, (h + 1) * each - HEAD_DIM : (h + 1) * each]
            for h in range(heads)
        ]
        values_ref[:, row : row + block] = jnp.concatenate(vals, axis=1).astype(F32).T.astype(BF)
    for row in range(0, rows, block):
        end = row + block
        first = first_ref[:, row:end]
        outs = []
        for h in range(heads):
            c = h * each
            queries = qkv_ref[row:end, c : c + HEAD_DIM] * scale
            keys = qkv_ref[:end, c + HEAD_DIM : c + 2 * HEAD_DIM]
            scores = masked(contract(keys, queries, 1, 1), first, row)
            peak = jnp.max(scores[-1], axis=0, keepdims=True)
            if row:
                peak = jnp.maximum(peak, jnp.max(scores[0], axis=0, keepdims=True))
            exponents = [jnp.exp(part - peak) for part in scores]
            sums = sum(jnp.sum(part, axis=0, keepdims=True) for part in exponents)
            values = values_ref[h * HEAD_DIM : (h + 1) * HEAD_DIM, :end]
            low = join([part.astype(BF) for part in exponents])
            outs.append(contract(values, low, 1, 0) / sums)
            lse_ref[h : h + 1, row:end] = peak + jnp.log(sums)
        d = relative_block(place_ref, row // each_rows, blocks)
        at = row % each_rows
        att_ref[d, at : at + block, :] = jnp.concatenate(outs, axis=0).T.astype(BF)


def backward_kernel(head, place_ref, qkv_ref, att_ref, lse_ref, first_ref, *refs):
    grads_in, (out_ref, keys_ref, sum_ref, grad_ref) = refs[:-4], refs[-4:]
    blocks, each_rows = att_ref.shape[:2]
    rows = blocks * each_rows
    block = query_block(each_rows)
    scale = jnp.asarray(HEAD_DIM**-0.5, BF)
    c = head * 3 * HEAD_DIM
    e = head * HEAD_DIM
    for d, block_ref in enumerate(grads_in):
        grad_ref[d] = block_ref[:, e : e + HEAD_DIM]
    for row in range(0, rows, block):
        keys = qkv_ref[row : row + block, c + HEAD_DIM : c + 2 * HEAD_DIM] * scale
        keys_ref[:, row : row + block] = keys.astype(F32).T.astype(BF)
    sum_ref[...] = jnp.zeros_like(sum_ref)
    zero = jnp.zeros((block, HEAD_DIM), BF)
    for row in range(rows - block, -1, -block):
        end = row + block
        d = relative_block(place_ref, row // each_rows, blocks)
        at = row % each_rows
        queries = qkv_ref[row:end, c : c + HEAD_DIM] * scale
        keys = qkv_ref[:end, c + HEAD_DIM : c + 2 * HEAD_DIM]
        values = qkv_ref[:end, c + 2 * HEAD_DIM : c + 3 * HEAD_DIM]
        grad = grad_ref[d, at : at + block, :]
        att = att_ref[d, at : at + block, e : e + HEAD_DIM]
        delta = jnp.sum((grad.astype(F32) * att.astype(F32)).T, axis=0, keepdims=True)
        scores = masked(contract(keys, queries, 1, 1), first_ref[:, row:end], row)
        lse = lse_ref[head : head + 1, row:end]
        probs = join([jnp.exp(part - lse) for part in scores])
        grad_scores = (probs * (contract(values, grad, 1, 1) - delta)).astype(BF)
        grad_queries = contract(keys_ref[:, :end], grad_scores, 1, 0)
        out_ref[row:end, :HEAD_DIM] = grad_queries.T.astype(BF)
        right = jnp.concatenate(
            [
                jnp.concatenate([queries, zero], axis=1),
                jnp.concatenate([zero, grad], axis=1),
            ],
            axis=0,
        )
        left = jnp.concatenate([grad_scores, probs.astype(BF)], axis=1)
        sum_ref[:end, :] += jnp.dot(left, right, preferred_element_type=F32)
    out_ref[:, HEAD_DIM:] = sum_ref[...].astype(BF)


def kernel_call(kernel, out_shape, scratch_shapes, flops, place, *args):
    whole = pl.BlockSpec(memory_space=pltpu.VMEM)
    return pl.pallas_call(
        kernel,
        out_shape=out_shape,
        in_specs=[pl.BlockSpec(memory_space=pltpu.SMEM)] + [whole] * len(args),
        out_specs=jax.tree.map(lambda _: whole, out_shape),
        scratch_shapes=scratch_shapes,
        compiler_params=pltpu.CompilerParams(vmem_limit_bytes=48 * 2**20),
        cost_estimate=pl.CostEstimate(
            flops=flops, bytes_accessed=sum(a.size * 2 for a in args), transcendentals=flops // 64
        ),
    )(place, *args)


def attend_forward(place, qkv, first, blocks):
    rows, width = qkv.shape
    shapes = (
        jax.ShapeDtypeStruct((blocks, rows // blocks, width // 3), BF),
        jax.ShapeDtypeStruct((8 * pl.cdiv(width // (3 * HEAD_DIM), 8), rows), F32),
    )
    scratch = [pltpu.VMEM((width // 3, rows), BF)]
    flops = 8 * rows * rows * width // 3
    return kernel_call(forward_kernel, shapes, scratch, flops, place, qkv, first)


def attend_backward(head, place, qkv, att, lse, first, grads):
    blocks, each_rows = att.shape[:2]
    rows = qkv.shape[0]
    shape = jax.ShapeDtypeStruct((rows, 3 * HEAD_DIM), BF)
    scratch = [
        pltpu.VMEM((HEAD_DIM, rows), BF),
        pltpu.VMEM((rows, 2 * HEAD_DIM), F32),
        pltpu.VMEM((blocks, each_rows, HEAD_DIM), BF),
    ]
    flops = 2 * rows * rows * HEAD_DIM
    kernel = partial(backward_kernel, head)
    return kernel_call(kernel, shape, scratch, flops, place, qkv, att, lse, first, *grads)


def dp_bits():
    return (lax.axis_size("dp") - 1).bit_length()


def doubles():
    size = lax.axis_size("dp")
    return size == 1 << dp_bits() and 1 < size <= 8


def relative_blocks():
    size = lax.axis_size("dp")
    pos = jnp.arange(size, dtype=jnp.int32)
    if not doubles():
        return pos
    high = dp_bits() - 1
    return ((pos & ((1 << high) - 1)) << 1 | pos >> high) ^ lax.axis_index("dp")


def chosen_columns(width):
    each = width // lax.axis_size("dp")
    source = (relative_blocks()[:, None] * each + jnp.arange(each, dtype=jnp.int32)).reshape(-1)
    return (jnp.arange(width, dtype=jnp.int32)[:, None] == source[None, :]).astype(BF)


def flip(value, axis, bit):
    size = lax.axis_size(axis)
    return lax.ppermute(value, axis, [(i, i ^ (1 << bit)) for i in range(size)])


def after(value, other):
    return lax.optimization_barrier((value, other))[0]


def exchange(blocks):
    size = lax.axis_size("tensor")
    came = [
        lax.ppermute(blocks[d], "tensor", [(i, (i + d) % size) for i in range(size)])
        for d in range(1, size)
    ]
    return [blocks[0]] + came[::-1]


def fold(rows, width):
    groups = width // rows.shape[-1]
    each = rows.shape[-2] // groups
    return jnp.concatenate(
        [rows[..., g * each : (g + 1) * each, :] for g in range(groups)], axis=-1
    )


def unfold(rows, width):
    groups = rows.shape[-1] // width
    return jnp.concatenate([rows[..., g * width : (g + 1) * width] for g in range(groups)], axis=-2)


class Doubling:
    def __init__(self, block, upward):
        high = list(range(1, dp_bits()))
        self.block, self.shape, self.held, self.came = block, block.shape, [], None
        self.bits = (high if upward else high[::-1]) + [0] if doubles() else []

    def start(self):
        self.came = flip(self.block, "dp", self.bits[0]) if self.bits else self.block

    def step(self):
        if self.bits:
            bit = self.bits.pop(0)
            at = 1 + sum(b > bit for b in self.held) if bit else 1
            came = flip(self.block, "dp", bit) if self.came is None else self.came
            self.came = None
            self.block = jnp.stack([self.block, came], axis=at)
            self.held.append(bit)

    def result(self):
        while self.bits:
            self.step()
        if not self.held:
            return lax.all_gather(self.block, "dp", axis=1)
        return self.block.reshape(self.shape[0], lax.axis_size("dp"), *self.shape[1:])


class Halving:
    def __init__(self, parts, upward):
        bits = dp_bits()
        high = list(range(1, bits))
        self.block, self.bits, self.axes = parts, [], None
        if doubles():
            self.block = parts.reshape(parts.shape[0], *[2] * bits, *parts.shape[2:])
            self.bits = [0] + (high[::-1] if upward else high)
            self.axes = {0: 1, **{b: 1 + bits - b for b in high}}

    def step(self):
        if self.bits:
            bit = self.bits.pop(0)
            at = self.axes[bit]
            keep = lax.index_in_dim(self.block, 0, at, keepdims=False)
            came = flip(lax.index_in_dim(self.block, 1, at, keepdims=False), "dp", bit)
            self.block = (keep.astype(F32) + came.astype(F32)).astype(BF)
            self.axes = {b: a - (a > at) for b, a in self.axes.items()}

    def result(self):
        if self.axes is None:
            return lax.psum_scatter(self.block, "dp", scatter_dimension=1)
        while self.bits:
            self.step()
        return self.block


def total(vector, axis):
    for bit in range((lax.axis_size(axis) - 1).bit_length()):
        vector = vector + flip(vector, axis, bit)
    return vector


def on_device(
    inputs,
    lengths,
    w_qkv,
    b_qv,
    w_out,
    b_out,
    w_fc,
    b_fc,
    w_proj,
    b_proj,
    gain_one,
    shift_one,
    gain_two,
    shift_two,
    cotangent,
):
    row_count, model_width = inputs.shape[1:]
    tensor_size = lax.axis_size("tensor")
    dp_size = lax.axis_size("dp")
    tensor_pos = lax.axis_index("tensor")
    pack_len = row_count * tensor_size
    head_width = w_qkv.shape[2]
    local_heads = head_width // HEAD_DIM
    fc_local = b_fc.shape[0]
    owned = model_width // dp_size
    out_rows = owned * head_width // fc_local
    place = chosen_columns(model_width)

    def relative(rows):
        return jnp.dot(rows, place, preferred_element_type=F32)

    def absolute(rows):
        return jnp.einsum(
            "td,cd->tc",
            rows,
            place.astype(rows.dtype),
            precision=lax.Precision.HIGHEST,
            preferred_element_type=F32,
        )

    qkv_rows = w_qkv.reshape(3, owned, local_heads, HEAD_DIM).transpose(1, 2, 0, 3)
    qkv_full = Doubling(qkv_rows.reshape(1, owned, 3 * head_width), True).result()
    vectors = relative(jnp.stack([gain_one, shift_one, gain_two, shift_two, b_out, b_proj]))
    gain_first, shift_first, gain_second, shift_second, bias_out, bias_proj = vectors
    rows_in = relative(inputs[0])
    normed_one, _ = norm_parts(rows_in)
    h_one = (normed_one * gain_first + shift_first).astype(BF)
    h_one_all = lax.all_gather(h_one, "tensor", axis=0, tiled=True)

    shard = jnp.concatenate([w_fc, w_proj.T, fold(w_out.T, fc_local), b_fc[None]])
    shards = exchange([shard] * tensor_size)
    shards, qkv_full = lax.optimization_barrier((shards, qkv_full))
    qkv_full = qkv_full.reshape(model_width, 3 * head_width)

    bias_fc = jnp.stack([part[-1:] for part in shards]).astype(F32)
    outs = [unfold(part[2 * owned : -1], head_width) for part in shards]
    gathers = [
        Doubling(jnp.stack([part[:owned] for part in shards]), True),
        Doubling(jnp.stack([part[owned : 2 * owned] for part in shards]), False),
        Doubling(jnp.concatenate(outs, axis=1)[None], True),
    ]
    for gather in gathers:
        gather.step()
    held = lax.optimization_barrier([g.block for g in gathers])
    for gather, block in zip(gathers, held):
        gather.block = block

    place_on_line = tensor_pos.astype(jnp.int32).reshape(1)
    first = first_allowed(lengths[0, 0], pack_len)
    none = jnp.zeros_like(b_qv[0])
    bias_qkv = jnp.stack([b_qv[0], none, b_qv[1]]).astype(F32)
    bias_qkv = bias_qkv.reshape(3, local_heads, HEAD_DIM).transpose(1, 0, 2).reshape(-1)
    projected = jnp.dot(h_one_all, qkv_full, preferred_element_type=F32)
    qkv = (projected + bias_qkv).astype(BF)
    att_all, lse = attend_forward(place_on_line, qkv, first, tensor_size)
    for gather in gathers:
        gather.start()
    att_all, held = lax.optimization_barrier((att_all, [g.came for g in gathers]))
    for gather, came in zip(gathers, held):
        gather.came = came
        gather.step()
    att = exchange([att_all[d] for d in range(tensor_size)])
    att, held = lax.optimization_barrier((att, [g.block for g in gathers]))
    for gather, block in zip(gathers, held):
        gather.block = block
    att_rows = jnp.concatenate(att, axis=1)
    fc_full, proj_t, out_t = [gather.result() for gather in gathers]
    fc_full = fc_full.reshape(tensor_size, model_width, fc_local)
    proj_t = proj_t.reshape(tensor_size, model_width, fc_local)
    out_t = out_t.reshape(model_width, model_width)

    middle = (
        rows_in + jnp.einsum("tc,dc->td", att_rows, out_t, preferred_element_type=F32) + bias_out
    )
    normed_two, inverse_two = norm_parts(middle)
    h_two = (normed_two * gain_second + shift_second).astype(BF)
    pre_act = jnp.einsum("td,zdf->ztf", h_two, fc_full, preferred_element_type=F32) + bias_fc
    root = (2.0 / jnp.pi) ** 0.5
    bend = jnp.tanh(root * (pre_act + 0.044715 * pre_act * pre_act * pre_act))
    active = (0.5 * pre_act * (1.0 + bend)).astype(BF)
    slope = 0.5 * (1.0 + bend) + 0.5 * pre_act * (1.0 - bend * bend) * root * (
        1.0 + 3 * 0.044715 * pre_act * pre_act
    )
    grad_y = relative(cotangent[0])
    grad_low = grad_y.astype(BF)
    grad_active = jnp.einsum("td,zdf->ztf", grad_low, proj_t, preferred_element_type=F32)
    grad_pre = (grad_active * slope).astype(BF)
    grad_h_two = jnp.einsum("ztf,zdf->td", grad_pre, fc_full, preferred_element_type=F32)
    grad_middle = grad_y + norm_back(grad_h_two * gain_second, normed_two, inverse_two)
    grad_branch = grad_middle.astype(BF)
    grad_att_rows = jnp.dot(grad_branch, out_t, preferred_element_type=F32).astype(BF)
    grad_att = exchange(
        [grad_att_rows[:, d * head_width : (d + 1) * head_width] for d in range(tensor_size)]
    )


    def by_owner(left, right):
        full = jnp.einsum("td,ztf->zdf", left, right, preferred_element_type=F32).astype(BF)
        return full.reshape(tensor_size, dp_size, owned, fc_local)

    d_out_all = jnp.einsum(
        "td,tc->dc", grad_branch, att_rows, preferred_element_type=F32
    )
    parts = [
        Halving(by_owner(h_two, grad_pre), True),
        Halving(by_owner(grad_low, active), False),
        Halving(d_out_all.astype(BF).reshape(1, dp_size, owned, model_width), True),
    ]
    for part in parts:
        part.step()

    early_rows = jnp.stack(
        [
            jnp.sum(grad_h_two * normed_two, axis=0),
            jnp.sum(grad_h_two, axis=0),
            jnp.sum(grad_middle, axis=0),
            jnp.sum(grad_y, axis=0),
        ]
    )
    sums_fc = jnp.sum(grad_pre, axis=1, dtype=F32)

    by_head = []
    for head in range(local_heads):
        by_head.append(attend_backward(head, place_on_line, qkv, att_all, lse, first, grad_att))
        if head == 0:
            grad_att, held, by_head[0] = lax.optimization_barrier(
                (grad_att, [part.block for part in parts], by_head[0])
            )
            for part, block in zip(parts, held):
                part.block = block
                part.step()
    stacked = jnp.concatenate(by_head, axis=1)

    def tied(values):
        values, held = lax.optimization_barrier((values, [part.block for part in parts]))
        for part, block in zip(parts, held):
            part.block = block
        return values

    qkv_absolute = jnp.dot(place, qkv_full, preferred_element_type=F32).astype(BF)
    grad_middle = absolute(grad_middle)
    terms = jnp.einsum("te,ce->tc", stacked, qkv_absolute, preferred_element_type=F32).astype(BF)
    grad_h_one = lax.psum_scatter(terms, "tensor", scatter_dimension=0, tiled=True).astype(F32)
    stacked, grad_middle, terms = tied((stacked, grad_middle, terms))
    for part in parts:
        part.step()
    stacked = tied(stacked)
    mlp_out = jnp.einsum("ztf,zdf->td", after(active, terms), proj_t, preferred_element_type=F32)
    output = absolute((middle + mlp_out + bias_proj).astype(BF)).astype(BF)

    sums_fc_w, sums_proj_w, sums_out_w = [part.result() for part in parts]
    pieces = [
        jnp.concatenate(
            [
                sums_fc_w[d],
                sums_proj_w[d],
                fold(sums_out_w[0, :, d * head_width : (d + 1) * head_width], fc_local),
            ]
        )
        for d in range(tensor_size)
    ]
    pieces = exchange(pieces)

    sums = jnp.sum(stacked, axis=0, dtype=F32)
    sums_by = sums.reshape(local_heads, 3, HEAD_DIM).transpose(1, 0, 2).reshape(3, head_width)
    sum_qv = sums_by[0::2]
    qkv_all = jnp.einsum(
        "td,te->de",
        h_one_all,
        stacked,
        preferred_element_type=F32,
    )
    wide_weights = qkv_full.astype(F32)
    normed_sums = (qkv_all - shift_first[:, None] * sums[None, :]) / gain_first[:, None]
    late_rows = jnp.stack(
        [
            jnp.sum(wide_weights * normed_sums, axis=1),
            jnp.sum(wide_weights * sums[None, :], axis=1),
        ]
    )
    d_qkv = Halving(qkv_all.astype(BF).reshape(1, dp_size, owned, 3 * head_width), True)
    d_qkv = d_qkv.result()[0]
    d_qkv = d_qkv.astype(F32).reshape(owned, local_heads, 3, HEAD_DIM).transpose(2, 0, 1, 3)
    d_qkv = d_qkv.reshape(3, owned, head_width)

    normed_rows, inverse_rows = norm_parts(inputs[0].astype(F32))
    grad_in = grad_middle + norm_back(
        grad_h_one * gain_one.astype(F32), normed_rows, inverse_rows
    )
    wide = model_width
    placed_fc = lax.dynamic_update_slice(
        jnp.zeros((2 * tensor_size, fc_local), F32), sums_fc, (tensor_pos, 0)
    )
    placed_fc = placed_fc[:tensor_size] + placed_fc[tensor_size:]
    rows = absolute(jnp.concatenate([early_rows, late_rows])).reshape(-1)
    sums_all = total(
        jnp.concatenate([rows, placed_fc.reshape(-1), sum_qv.reshape(-1)]), "dp"
    )
    sum_qv = sums_all[rows.size + placed_fc.size :].reshape(2, head_width)
    sums_all, pieces[1::2], d_qkv = lax.optimization_barrier(
        (sums_all[: rows.size + placed_fc.size], pieces[1::2], d_qkv)
    )
    sums_all = total(sums_all, "tensor")
    d_shard = sum(came.astype(F32) for came in pieces)
    d_fc = d_shard[:owned]
    d_proj = d_shard[owned : 2 * owned].T
    d_out = unfold(d_shard[2 * owned :], head_width).T
    d_gain_two, d_shift_two, d_b_out, d_b_proj, d_gain_one, d_shift_one = (
        sums_all[: 6 * wide].reshape(6, wide)
    )
    d_b_fc = lax.dynamic_slice(sums_all[6 * wide :], (tensor_pos * fc_local,), (fc_local,))
    return (
        output[None],
        grad_in[None],
        d_qkv,
        sum_qv,
        d_out,
        d_b_out,
        d_fc,
        d_b_fc,
        d_proj,
        d_b_proj,
        d_gain_one,
        d_shift_one,
        d_gain_two,
        d_shift_two,
    )


def solution(mesh):
    rows = P(None, ("dp", "tensor"), None)
    placed = (
        rows,
        P("dp", None, None),
        P(None, "dp", "tensor"),
        P(None, "tensor"),
        P("tensor", "dp"),
        P(),
        P("dp", "tensor"),
        P("tensor"),
        P("tensor", "dp"),
        P(),
        P(),
        P(),
        P(),
        P(),
        rows,
    )
    return jax.shard_map(
        on_device,
        mesh=mesh,
        in_specs=placed,
        out_specs=(
            rows,
            rows,
            P(None, "dp", "tensor"),
            P(None, "tensor"),
            P("tensor", "dp"),
            P(),
            P("dp", "tensor"),
            P("tensor"),
            P("tensor", "dp"),
            P(),
            P(),
            P(),
            P(),
            P(),
        ),
        check_vma=False,
    )
```
